32 devices in a mesh: ctx: 8 (over z, y), mp: 4 (over x, core).
Axes of the slice: x: 2, y: 2, z: 4, core: 2. Of those that a mesh axis runs over, the one named last changes fastest.
Arguments:
- q_mr: bfloat16 [2048, 4096], P('ctx', 'mp'), may hold values from -6 to 6
- k_mr: bfloat16 [2048, 4096], P('ctx', 'mp'), may hold values from -6 to 6
- v_mr: bfloat16 [2048, 4096], P('ctx', 'mp'), may hold values from -6 to 6
- q_li: bfloat16 [2048, 4096], P('ctx', 'mp'), may hold values from -6 to 6
- k_li: bfloat16 [2048, 4096], P('ctx', 'mp'), may hold values from -6 to 6
- short_taps: float32 [6, 3, 4096], P(None, None, 'mp'), may hold values from -3.5 to 3.5
- mr_taps: float32 [128, 4096], P(None, 'mp'), may hold values from -0.5 to 0.5
- norm_gain: float32 [4096], P('mp'), may hold values from 0.1 to 1.9
- decay_rate: float32 [16, 4096], P(None, 'mp'), may hold values from 0.00014648438 to 0.03
- residue: float32 [16, 4096], P(None, 'mp'), may hold values from -1.5 to 1.5
Outputs:
- mixer_mr: bfloat16 [2048, 4096], P('ctx', 'mp')
- mixer_li: bfloat16 [2048, 4096], P('ctx', 'mp')
The draws below stay inside these ranges and needn't reach their ends.
All inputs are finite; a program needn't handle non-finite values.
Results may differ from the reference program's by a relative error of at most 0.0078.
Values may be sent and summed in bfloat16 or wider, within the bound.
A program may use at most 64 MiB of HBM per device.

```python
import math
import jax
import jax.numpy as jnp
from jax import lax

D = 4096
FILT = 128
SHORT = 3
MODES = 16
SEQ = 2048


def levels(key, shape, split, low, high):
    def one(axis_at, parts):
        draws = jax.random.uniform(jax.random.fold_in(jax.random.fold_in(key, 6), axis_at), (parts,), jnp.float32, low / len(split), high / len(split))
        return jnp.repeat(jnp.exp(draws), shape[axis_at] // parts).reshape((-1,) + (1,) * (len(shape) - axis_at - 1))

    gain = one(*split[0])
    for cut in split[1:]:
        gain = gain * one(*cut)
    return gain


def normal_values(stream_key, dims, scale, most, shards=(), kind=jnp.bfloat16):
    values = jax.random.normal(stream_key, dims, jnp.float32) * scale
    if len(shards) > 0:
        values = levels(stream_key, dims, shards, -0.22, 0.18) * values
    return jnp.clip(values, min=-most, max=most).astype(kind)


def setup_inputs(seed: int = 0) -> dict:
    splits = jax.random.split(jax.random.key(seed), 11)
    q_mr = normal_values(splits[0], (SEQ, D), 1.0, 6.0, ((0, 8), (1, 4)))
    k_mr = normal_values(splits[1], (SEQ, D), 1.0, 6.0, ((0, 8), (1, 4)))
    v_mr = normal_values(splits[2], (SEQ, D), 1.0, 6.0, ((0, 8), (1, 4)))
    q_li = normal_values(splits[3], (SEQ, D), 1.0, 6.0, ((0, 8), (1, 4)))
    k_li = normal_values(splits[4], (SEQ, D), 1.0, 6.0, ((0, 8), (1, 4)))
    short_taps = normal_values(splits[5], (6, SHORT, D), SHORT ** -0.5, 3.5, ((2, 4),), jnp.float32)
    mr_taps = normal_values(splits[6], (FILT, D), FILT ** -0.5, 0.5, ((1, 4),), jnp.float32)
    norm_gain = jnp.clip(1.0 + 0.18 * jax.random.normal(splits[7], (D,), jnp.float32), 0.1, 1.9)
    decay_rate = jnp.clip(jnp.exp(math.log(0.03) - 5.322034 * jax.random.uniform(splits[8], (MODES, D), jnp.float32) ** levels(splits[8], (MODES, D), ((1, 4),), -0.2, 0.2)), 0.00014648438, 0.03)
    residue = normal_values(splits[9], (MODES, D), 0.25, 1.5, ((1, 4),), jnp.float32)
    return {"q_mr": q_mr, "k_mr": k_mr, "v_mr": v_mr, "q_li": q_li, "k_li": k_li, "short_taps": short_taps, "mr_taps": mr_taps, "norm_gain": norm_gain, "decay_rate": decay_rate, "residue": residue}


def settle(values):
    return lax.optimization_barrier(values.astype(jnp.bfloat16))

def lag_conv(stream, taps):
    length = stream.shape[0]
    width = taps.shape[0]
    padded = jnp.pad(stream, ((width - 1, 0), (0, 0)))

    def add_lag(total, pair):
        lag, tap = pair
        start = (width - 1 - lag).astype(jnp.int32)
        piece = lax.dynamic_slice_in_dim(padded, start, length, 0)
        return (total + tap[None, :] * piece, None)
    lags = jnp.arange(width).astype(jnp.int32)
    total, _ = lax.scan(add_lag, jnp.zeros(stream.shape, jnp.float32).astype(stream.dtype), (lags, taps))
    return total

def short_conv(stream, taps):
    return lag_conv(stream.astype(jnp.float32), taps)

def mode_weight(rate, res):
    return res * jnp.sqrt(-jnp.expm1(-2.0 * rate))

def filter_table(rate, residue, length):
    times = jnp.arange(length).astype(jnp.float32)[:, None]

    def add_mode(total, pair):
        one_rate, one_res = pair
        return (total + mode_weight(one_rate, one_res)[None, :] * jnp.exp(-one_rate[None, :] * times), None)
    start = jnp.zeros((length, rate.shape[1]), jnp.float32)
    table, _ = lax.scan(add_mode, start, (rate, residue))
    return table

def block_ends(blocks, rate):
    length = blocks.shape[1]
    lags = (length - 1 - jnp.arange(length)).astype(jnp.float32)[:, None]

    def one_mode(carry, one_rate):
        return (carry, lax.optimization_barrier(jnp.sum(blocks * jnp.exp(-one_rate[None, :] * lags)[None], axis=1)))
    _, ends = lax.scan(one_mode, jnp.zeros((), jnp.float32), rate)
    return jnp.swapaxes(ends, 0, 1)

def carried_terms(starts, rate, residue, length):
    times = (jnp.arange(length) + 1).astype(jnp.float32)[:, None]

    def add_mode(total, triple):
        one_rate, one_res, state = triple
        factor = mode_weight(one_rate, one_res)[None, :] * jnp.exp(-one_rate[None, :] * times)
        return (total + factor[None] * state[:, None, :], None)
    start = jnp.zeros((starts.shape[0], length, rate.shape[1]), jnp.float32)
    total, _ = lax.scan(add_mode, start, (rate, residue, jnp.swapaxes(starts, 0, 1)))
    return total

def reference(q_mr, k_mr, v_mr, q_li, k_li, short_taps, mr_taps, norm_gain, decay_rate, residue):
    sq = short_conv(q_mr, short_taps[0])
    sk = short_conv(k_mr, short_taps[1])
    sv = short_conv(v_mr, short_taps[2])
    u_mr = settle(sk * sv)
    mr_long = lag_conv(u_mr.astype(jnp.float32), mr_taps)
    mixer_mr = (sq * mr_long).astype(jnp.bfloat16)
    wide = mixer_mr.astype(jnp.float32)
    mean_sq = lax.optimization_barrier(jnp.mean(wide * wide, axis=1, keepdims=True))
    normed = settle(wide * lax.rsqrt(mean_sq + 1e-06) * norm_gain[None, :])
    lq = short_conv(q_li, short_taps[3])
    lk = short_conv(k_li, short_taps[4])
    lv = short_conv(normed, short_taps[5])
    u_li = settle(lk * lv)
    ref_block = 32
    blocks = u_li.astype(jnp.float32).reshape(SEQ // ref_block, ref_block, D)
    table = filter_table(decay_rate, residue, ref_block)
    lag = (jnp.arange(ref_block)[:, None] - jnp.arange(ref_block)[None, :]).astype(jnp.int32)
    picked = jnp.take(table, jnp.clip(lag, 0, ref_block - 1), axis=0)
    toeplitz = jnp.where((lag >= 0)[:, :, None], picked, jnp.zeros_like(picked))
    decay = jnp.exp(-decay_rate * ref_block)

    def advance(state, block):
        single = block[None]
        local = jnp.einsum('ijc,jc->ic', toeplitz, block, precision=lax.Precision.HIGHEST)
        carried = carried_terms(state[None], decay_rate, residue, ref_block)[0]
        ends = block_ends(single, decay_rate)[0]
        return (decay * state + ends, local + carried)
    _, outputs = lax.scan(advance, jnp.zeros((MODES, D), jnp.float32), blocks)
    long_li = settle(outputs.reshape(SEQ, D))
    mixer_li = (lq * long_li.astype(jnp.float32)).astype(jnp.bfloat16)
    return (mixer_mr, mixer_li)
```

```python
import functools

import jax
import jax.numpy as jnp
import numpy as np
from jax import lax
from jax.experimental import pallas as pl
from jax.experimental.pallas import tpu as pltpu
from jax.sharding import PartitionSpec as P

MESH = pl.DeviceIdType.MESH
BF = jnp.bfloat16
F32 = jnp.float32


def two_parts(m):
    hi = np.asarray(m, np.float32).astype(BF)
    lo = (np.asarray(m, np.float64) - hi.astype(np.float64)).astype(BF)
    return hi, lo


def dft_tables(length, first_out, n_in):
    half = length // 2
    k = np.arange(half)[:, None]
    t = np.arange(length)[None, :]
    ang = 2 * np.pi * ((k * t) % length) / length
    cos, sin = np.cos(ang), -np.sin(ang)
    sin[0] = (-1.0) ** np.arange(length)
    forward = np.concatenate([cos, sin], 0)
    wc, ws = 2 * cos, 2 * sin
    wc[0] = 1.0
    ws[0] = (-1.0) ** np.arange(length)
    inverse = np.concatenate([wc, ws], 0).T / length
    return two_parts(forward[:, :n_in]), two_parts(inverse[first_out:])


def dot(a, b):
    return jnp.dot(a, b, preferred_element_type=F32)


def split(x):
    hi = x.astype(BF)
    return hi, (x - hi.astype(F32)).astype(BF)


def dot3(ah, al, x):
    hi, lo = split(x)
    return dot(ah, hi) + dot(ah, lo) + dot(al, hi)


def conv3(x, rim8, taps):
    ext = jnp.concatenate([rim8, x], axis=0)
    x1 = pltpu.roll(ext, 1, 0)[8:]
    x2 = pltpu.roll(ext, 2, 0)[8:]
    return taps[0:1] * x + taps[1:2] * x1 + taps[2:3] * x2


def spectrum_product(u, h, half):
    ur, ui = u[:half], u[half:]
    hr, hi, hn = h[:half], h[half : 2 * half], h[2 * half :]
    hr2 = jnp.concatenate([hn, hr[8:]], axis=0)
    return jnp.concatenate([ur * hr - ui * hi, ur * hi + ui * hr2], axis=0)


def store_spectrum(ref, h, half, cols):
    top = lax.broadcasted_iota(jnp.int32, (8, h.shape[1]), 0) == 0
    hr, hi = h[:half], h[half:]
    ref[0:half, cols] = hr
    ref[half : half + 8, cols] = jnp.where(top, 0.0, hi[:8])
    ref[half + 8 : 2 * half, cols] = hi[8:]
    ref[2 * half : 2 * half + 8, cols] = jnp.where(top, hi[:8], hr[:8])


def kernel(
    n, mp, q_mr, k_mr, v_mr, q_li, k_li, short, mr_taps, gain, rate, res, f1h, f1l, g1h, g1l, f2h, f2l, g2h, g2l,
    out_mr, out_li,
    u_own, u_halo, pack, rims, spec1, spec2, hbuf, lkb, lqb, nbuf, nrim, u32, ylong, wgt, ebuf, carry, st, ss, scale, acc_ss,
    rim_s, rim_r, halo_s, halo_r, nr_s, nr_r, ss_s, ss_r, st_s, st_r,
):
    T, C = q_mr.shape
    H = T // 2
    modes = rate.shape[0]
    CW = 256
    chunks = C // CW
    ctx = lax.axis_index("ctx")
    mpi = lax.axis_index("mp")
    not_last = ctx < n - 1
    not_first = ctx > 0

    def cols_of(i, w=CW):
        return pl.ds(pl.multiple_of(i * w, w), w)

    def loop(count, body):
        def step(i, c):
            body(i)
            return c

        lax.fori_loop(0, count, step, 0)

    barrier = pltpu.get_barrier_semaphore()

    def greet(j, c):
        pl.semaphore_signal(barrier, inc=1, device_id={"ctx": lax.rem(ctx + j, n)}, device_id_type=MESH)
        return c

    lax.fori_loop(1, n, greet, 0)
    for j in range(1, mp):
        pl.semaphore_signal(barrier, inc=1, device_id={"mp": lax.rem(mpi + j, mp)}, device_id_type=MESH)

    def pack_body(i):
        cols = cols_of(i)
        row = lax.broadcasted_iota(jnp.int32, (8, CW), 0)
        first = jnp.zeros((8, CW), F32)
        second = jnp.zeros((8, CW), F32)
        for s, stream in enumerate((q_mr, k_mr, v_mr, q_li, k_li)):
            tail = stream[T - 16 : T, cols].astype(F32)[8:]
            moved = pltpu.roll(tail, (2 + 2 * s) % 8, 0) if (2 + 2 * s) % 8 else tail
            here = (row >= (2 * s) % 8) & (row < (2 * s) % 8 + 2)
            if s < 4:
                first = jnp.where(here, moved, first)
            else:
                second = jnp.where(here, moved, second)
        pack[:, cols] = jnp.concatenate([first, second], axis=0).astype(BF)

    loop(chunks, pack_body)

    @pl.when(jnp.logical_not(not_first))
    def _():
        rims[...] = jnp.zeros(rims.shape, BF)
        nrim[...] = jnp.zeros(nrim.shape, BF)
        u_halo[...] = jnp.zeros(u_halo.shape, BF)

    def u_rows(lo, rows, cols, rim_k, rim_v):
        k = conv3(k_mr[lo : lo + rows, cols].astype(F32), rim_k, short[1, :, cols])
        v = conv3(v_mr[lo : lo + rows, cols].astype(F32), rim_v, short[2, :, cols])
        u_own[lo : lo + rows, cols] = (k * v).astype(BF)

    def before(stream, lo, cols):
        return stream[lo - 16 : lo, cols].astype(F32)[8:]

    def u_late(i):
        cols = cols_of(i)
        u_rows(H, H, cols, before(k_mr, H, cols), before(v_mr, H, cols))

    loop(chunks, u_late)

    pl.semaphore_wait(barrier, n - 1 + mp - 1)

    nxt = {"ctx": lax.rem(ctx + 1, n)}
    rim_copy = pltpu.make_async_remote_copy(pack, rims, rim_s, rim_r, device_id=nxt, device_id_type=MESH)
    halo_copy = pltpu.make_async_remote_copy(
        u_own.at[pl.ds(H, H)], u_halo, halo_s, halo_r, device_id=nxt, device_id_type=MESH
    )
    nr_copy = pltpu.make_async_remote_copy(
        nbuf.at[pl.ds(T - 16, 16)], nrim, nr_s, nr_r, device_id=nxt, device_id_type=MESH
    )

    @pl.when(not_last)
    def _():
        rim_copy.start()
        halo_copy.start()

    def mr_spec(i):
        cols = cols_of(i)
        store_spectrum(spec1, dot3(f1h[:, 0:H], f1l[:, 0:H], mr_taps[:, cols]), T // 2, cols)

    loop(chunks, mr_spec)

    @pl.when(not_first)
    def _():
        rim_copy.wait_recv()

    def rim_of(s, cols):
        both = rims[:, cols].astype(F32)
        part = both[0:8] if s < 4 else both[8:16]
        by = (6 - 2 * s) % 8
        return pltpu.roll(part, by, 0) if by else part

    def u_early(i):
        cols = cols_of(i)
        u_rows(0, H, cols, rim_of(1, cols), rim_of(2, cols))

    loop(chunks, u_early)

    def mr_half(part):
        acc_ss[...] = jnp.zeros(acc_ss.shape, F32)

        def body(i):
            cols = cols_of(i)
            if part == 1:
                win = u_own[:, cols]
                sq = conv3(q_mr[H:T, cols].astype(F32), before(q_mr, H, cols), short[0, :, cols])
            else:
                win = jnp.concatenate([u_halo[:, cols], u_own[0:H, cols]], axis=0)
                sq = conv3(q_mr[0:H, cols].astype(F32), rim_of(0, cols), short[0, :, cols])
            u = dot(f1h[...], win) + dot(f1l[...], win)
            y = dot3(g1h[...], g1l[...], spectrum_product(u, spec1[:, cols], T // 2))
            m = (sq * y).astype(BF)
            out_mr[part * H : part * H + H, cols] = m
            w = m.astype(F32)
            w = w * w
            acc_ss[...] += w[:, 0:128] + w[:, 128:256]

        loop(chunks, body)
        row = jnp.sum(acc_ss[...].T, axis=0, keepdims=True)
        ss[part, mpi] = jnp.broadcast_to(row, (8, H))

    def ss_copy(part, j, slot):
        return pltpu.make_async_remote_copy(
            ss.at[part, slot], ss.at[part, slot], ss_s.at[part, j], ss_r.at[part, slot],
            device_id={"mp": lax.rem(mpi + j, mp)}, device_id_type=MESH,
        )

    def ss_send(part):
        for j in range(1, mp):
            ss_copy(part, j, mpi).start()

    def norm_half(part):
        for j in range(1, mp):
            ss_copy(part, j, lax.rem(mpi + j, mp)).wait_recv()
        total = ss[part, 0]
        for j in range(1, mp):
            total = total + ss[part, j]
        sc = lax.rsqrt(total / (C * mp) + 1e-06)
        scale[...] = jnp.broadcast_to(sc[0:1], (H, H)).T

        def body(i):
            cols = cols_of(i)
            s = scale[...]
            s = jnp.concatenate([s, s], axis=1)
            m = out_mr[part * H : part * H + H, cols].astype(F32)
            nbuf[part * H : part * H + H, cols] = (m * s * gain[0:1, cols]).astype(BF)

        loop(chunks, body)

    mr_half(1)
    ss_send(1)

    def li_gates(i):
        cols = cols_of(i)
        lkb[:, cols] = conv3(k_li[:, cols].astype(F32), rim_of(4, cols), short[4, :, cols])
        lqb[:, cols] = conv3(q_li[:, cols].astype(F32), rim_of(3, cols), short[3, :, cols])

    loop(chunks, li_gates)

    norm_half(1)

    @pl.when(not_last)
    def _():
        nr_copy.start()

    x = 2.0 * rate[...]
    series = x * (1.0 + x * (-1.0 / 2 + x * (1.0 / 6 + x * (-1.0 / 24 + x * (1.0 / 120 - x * (1.0 / 720))))))
    wgt[...] = res[...] * jnp.sqrt(jnp.where(x < 0.125, series, 1.0 - jnp.exp(-x)))

    sub = lax.broadcasted_iota(jnp.int32, (8, 128), 0).astype(F32)

    def rows_of(ref, cols):
        return [jnp.broadcast_to(ref[m : m + 1, cols], (8, 128)) for m in range(modes)]

    def tree(vals):
        vals = list(vals)
        while len(vals) > 1:
            vals = [a + b for a, b in zip(vals[0::2], vals[1::2])] + ([vals[-1]] if len(vals) % 2 else [])
        return vals[0]

    def h_group(i):
        cols = cols_of(i, 128)
        r = rows_of(rate, cols)
        w = rows_of(wgt, cols)
        d8 = [jnp.exp(-8.0 * a) for a in r]
        g = tuple(b * jnp.exp(-a * sub) for a, b in zip(r, w))

        def step(k, g):
            hbuf[pl.ds(pl.multiple_of(k * 8, 8), 8), cols] = tree(g)
            return tuple(a * b for a, b in zip(g, d8))

        lax.fori_loop(0, T // 8, step, g, unroll=4)

    loop(C // 128, h_group)

    def li_spec(i):
        cols = cols_of(i)
        store_spectrum(spec2, dot3(f2h[...], f2l[...], hbuf[:, cols]), T, cols)

    loop(chunks, li_spec)

    @pl.when(not_first)
    def _():
        halo_copy.wait_recv()

    mr_half(0)
    ss_send(0)
    norm_half(0)

    @pl.when(not_first)
    def _():
        nr_copy.wait_recv()

    def li_u(i):
        cols = cols_of(i)
        lv = conv3(nbuf[:, cols].astype(F32), nrim[:, cols].astype(F32)[8:], short[5, :, cols])
        u32[:, cols] = (lkb[:, cols] * lv).astype(BF).astype(F32)

    loop(chunks, li_u)

    def ends_group(i):
        cols = cols_of(i, 128)
        r = rows_of(rate, cols)
        d8 = [jnp.exp(-8.0 * a) for a in r]

        def step(k, acc):
            u = u32[pl.ds(pl.multiple_of(k * 8, 8), 8), cols]
            return tuple(a * d + u for a, d in zip(acc, d8))

        acc = lax.fori_loop(0, T // 8, step, tuple(jnp.zeros((8, 128), F32) for _ in r), unroll=4)
        for m in range(modes):
            ebuf[m : m + 1, cols] = jnp.sum(acc[m] * jnp.exp(-r[m] * (7.0 - sub)), axis=0, keepdims=True)

    loop(C // 128, ends_group)
    st[ctx] = ebuf[...].astype(BF)

    def st_copy(dst, slot):
        return pltpu.make_async_remote_copy(
            st.at[slot], st.at[slot], st_s.at[dst], st_r.at[slot], device_id={"ctx": dst}, device_id_type=MESH
        )

    def st_start(j, c):
        st_copy(j, ctx).start()
        return c

    lax.fori_loop(ctx + 1, n, st_start, 0)

    def li_local(i):
        cols = cols_of(i)
        win = u32[:, cols].astype(BF)
        u = dot(f2h[...], win) + dot(f2l[...], win)
        ylong[:, cols] = dot3(g2h[...], g2l[...], spectrum_product(u, spec2[:, cols], T))

    loop(chunks, li_local)

    carry[...] = jnp.zeros(carry.shape, F32)

    def st_take(j, c):
        st_copy(lax.rem(ctx + 1, n), j).wait_recv()
        carry[...] = carry[...] * jnp.exp(-float(T) * rate[...]) + st[j].astype(F32)
        return c

    lax.fori_loop(0, ctx, st_take, 0)

    def out_group(i):
        cols = cols_of(i, 128)
        r = rows_of(rate, cols)
        w = rows_of(wgt, cols)
        s = rows_of(carry, cols)
        d8 = [jnp.exp(-8.0 * a) for a in r]
        g = tuple(b * c * jnp.exp(-a * (sub + 1.0)) for a, b, c in zip(r, w, s))

        def step(k, g):
            rows = pl.ds(pl.multiple_of(k * 16, 16), 16)
            y0 = tree(g)
            g = tuple(a * b for a, b in zip(g, d8))
            y1 = tree(g)
            g = tuple(a * b for a, b in zip(g, d8))
            y = ylong[rows, cols] + jnp.concatenate([y0, y1], axis=0)
            out_li[rows, cols] = (lqb[rows, cols] * y.astype(BF).astype(F32)).astype(BF)
            return g

        lax.fori_loop(0, T // 16, step, g, unroll=2)

    loop(C // 128, out_group)

    @pl.when(not_last)
    def _():
        rim_copy.wait_send()
        halo_copy.wait_send()
        nr_copy.wait_send()

    for part in range(2):
        for j in range(1, mp):
            ss_copy(part, j, mpi).wait_send()

    def st_end(j, c):
        st_copy(j, ctx).wait_send()
        return c

    lax.fori_loop(ctx + 1, n, st_end, 0)


def shards(n, mp, q_mr, k_mr, v_mr, q_li, k_li, short_taps, mr_taps, norm_gain, decay_rate, residue):
    T, C = q_mr.shape
    modes = decay_rate.shape[0]
    (f1h, f1l), (g1h, g1l) = dft_tables(T, T // 2, T)
    (f2h, f2l), (g2h, g2l) = dft_tables(2 * T, 0, T)
    g2h, g2l = g2h[:T], g2l[:T]
    tables = [jnp.asarray(a) for a in (f1h, f1l, g1h, g1l, f2h, f2l, g2h, g2l)]
    vm = pl.BlockSpec(memory_space=pltpu.VMEM)
    DMA = pltpu.SemaphoreType.DMA
    H = T // 2
    return pl.pallas_call(
        functools.partial(kernel, n, mp),
        out_shape=(jax.ShapeDtypeStruct((T, C), BF), jax.ShapeDtypeStruct((T, C), BF)),
        in_specs=[vm] * 18,
        out_specs=(vm, vm),
        scratch_shapes=[
            pltpu.VMEM((T, C), BF),
            pltpu.VMEM((H, C), BF),
            pltpu.VMEM((16, C), BF),
            pltpu.VMEM((16, C), BF),
            pltpu.VMEM((T + 8, C), F32),
            pltpu.VMEM((2 * T + 8, C), F32),
            pltpu.VMEM((T, C), F32),
            pltpu.VMEM((T, C), F32),
            pltpu.VMEM((T, C), F32),
            pltpu.VMEM((T, C), BF),
            pltpu.VMEM((16, C), BF),
            pltpu.VMEM((T, C), F32),
            pltpu.VMEM((T, C), F32),
            pltpu.VMEM((modes, C), F32),
            pltpu.VMEM((modes, C), F32),
            pltpu.VMEM((modes, C), F32),
            pltpu.VMEM((n, modes, C), BF),
            pltpu.VMEM((2, mp, 8, H), F32),
            pltpu.VMEM((H, H), F32),
            pltpu.VMEM((H, 128), F32),
            DMA, DMA, DMA, DMA, DMA, DMA,
            DMA((2, mp)), DMA((2, mp)), DMA((n,)), DMA((n,)),
        ],
        compiler_params=pltpu.CompilerParams(
            collective_id=0, has_side_effects=True, vmem_limit_bytes=40 * 1024 * 1024
        ),
    )(q_mr, k_mr, v_mr, q_li, k_li, short_taps, mr_taps, norm_gain[None], decay_rate, residue, *tables)


def solution(mesh):
    n, mp = mesh.shape["ctx"], mesh.shape["mp"]
    tok = P("ctx", "mp")
    in_specs = (tok,) * 5 + (P(None, None, "mp"), P(None, "mp"), P("mp"), P(None, "mp"), P(None, "mp"))
    return jax.shard_map(
        functools.partial(shards, n, mp), mesh=mesh, in_specs=in_specs, out_specs=(tok, tok), check_vma=False
    )
```

```python
import functools

import jax
import jax.numpy as jnp
import numpy as np
from jax import lax
from jax.experimental import pallas as pl
from jax.experimental.pallas import tpu as pltpu
from jax.sharding import PartitionSpec as P

MESH = pl.DeviceIdType.MESH
BF = jnp.bfloat16
IN = 15
ORDER = (1, 2, 5, 0, 3, 4, 6, 10, 11, 12, 13, 8, 9, 7, 14)
F32 = jnp.float32


def two_parts(m):
    hi = np.asarray(m, np.float32).astype(BF)
    lo = (np.asarray(m, np.float64) - hi.astype(np.float64)).astype(BF)
    return hi, lo


def dft_tables(length, first_out, n_in):
    half = length // 2
    k = np.arange(half)[:, None]
    t = np.arange(length)[None, :]
    ang = 2 * np.pi * ((k * t) % length) / length
    cos, sin = np.cos(ang), -np.sin(ang)
    sin[0] = (-1.0) ** np.arange(length)
    forward = np.concatenate([cos, sin], 0)
    wc, ws = 2 * cos, 2 * sin
    wc[0] = 1.0
    ws[0] = (-1.0) ** np.arange(length)
    inverse = np.concatenate([wc, ws], 0).T / length
    return two_parts(forward[:, :n_in]), two_parts(inverse[first_out:])


def dot(a, b):
    return jnp.dot(a, b, preferred_element_type=F32)


def split(x):
    hi = x.astype(BF)
    return hi, (x - hi.astype(F32)).astype(BF)


def dot3(ah, al, x):
    hi, lo = split(x)
    return dot(ah, hi) + dot(ah, lo) + dot(al, hi)


def conv3(x, rim8, taps):
    ext = jnp.concatenate([rim8, x], axis=0)
    x1 = pltpu.roll(ext, 1, 0)[8:]
    x2 = pltpu.roll(ext, 2, 0)[8:]
    return taps[0:1] * x + taps[1:2] * x1 + taps[2:3] * x2


def spectrum_product(u, h, half):
    ur, ui = u[:half], u[half:]
    hr, hi, hn = h[:half], h[half : 2 * half], h[2 * half :]
    hr2 = jnp.concatenate([hn, hr[8:]], axis=0)
    return jnp.concatenate([ur * hr - ui * hi, ur * hi + ui * hr2], axis=0)


def store_spectrum(ref, h, half, cols):
    top = lax.broadcasted_iota(jnp.int32, (8, h.shape[1]), 0) == 0
    hr, hi = h[:half], h[half:]
    ref[0:half, cols] = hr
    ref[half : half + 8, cols] = jnp.where(top, 0.0, hi[:8])
    ref[half + 8 : 2 * half, cols] = hi[8:]
    ref[2 * half : 2 * half + 8, cols] = jnp.where(top, hi[:8], hr[:8])


def kernel(
    n, mp, *refs,
):
    ins, refs = refs[:IN], refs[IN:]
    (out_mr, out_li), refs = refs[:2], refs[2:]
    vins, refs = refs[:IN], refs[IN:]
    q_mr, k_mr, v_mr, q_li, k_li, short, mr_taps, gain, rate, res, f1h, f1l, g1h, g1l, fcat = vins
    (load_s,
    u_own, u_halo, pack, rims, spec1, spec2, hbuf, lkb, lqb, nbuf, nrim, u32, ylong, wgt, ebuf, emid, late, carry, st, ss, scale, acc_ss,
    rim_s, rim_r, halo_s, halo_r, nr_s, nr_r, ss_s, ss_r, st_s, st_r) = refs
    loads = [pltpu.make_async_copy(a, b, load_s.at[i]) for i, (a, b) in enumerate(zip(ins, vins))]
    for i in ORDER:
        loads[i].start()

    def need(*which):
        for i in which:
            loads[i].wait()

    T, C = q_mr.shape
    H = T // 2
    modes = rate.shape[0]
    CW = 256
    chunks = C // CW
    ctx = lax.axis_index("ctx")
    mpi = lax.axis_index("mp")
    not_last = ctx < n - 1
    not_first = ctx > 0

    def cols_of(i, w=CW):
        return pl.ds(pl.multiple_of(i * w, w), w)

    def loop(count, body):
        def step(i, c):
            body(i)
            return c

        lax.fori_loop(0, count, step, 0)

    barrier = pltpu.get_barrier_semaphore()

    def greet(j, c):
        pl.semaphore_signal(barrier, inc=1, device_id={"ctx": lax.rem(ctx + j, n)}, device_id_type=MESH)
        return c

    lax.fori_loop(1, n, greet, 0)
    for j in range(1, mp):
        pl.semaphore_signal(barrier, inc=1, device_id={"mp": lax.rem(mpi + j, mp)}, device_id_type=MESH)

    def pack_body(i):
        cols = cols_of(i)
        row = lax.broadcasted_iota(jnp.int32, (8, CW), 0)
        first = jnp.zeros((8, CW), F32)
        second = jnp.zeros((8, CW), F32)
        for s, stream in enumerate((q_mr, k_mr, v_mr, q_li, k_li)):
            tail = stream[T - 16 : T, cols].astype(F32)[8:]
            moved = pltpu.roll(tail, (2 + 2 * s) % 8, 0) if (2 + 2 * s) % 8 else tail
            here = (row >= (2 * s) % 8) & (row < (2 * s) % 8 + 2)
            if s < 4:
                first = jnp.where(here, moved, first)
            else:
                second = jnp.where(here, moved, second)
        pack[:, cols] = jnp.concatenate([first, second], axis=0).astype(BF)

    need(0, 1, 2, 3, 4, 5)
    loop(chunks, pack_body)

    @pl.when(jnp.logical_not(not_first))
    def _():
        rims[...] = jnp.zeros(rims.shape, BF)
        nrim[...] = jnp.zeros(nrim.shape, BF)
        u_halo[...] = jnp.zeros(u_halo.shape, BF)

    def u_rows(lo, rows, cols, rim_k, rim_v):
        k = conv3(k_mr[lo : lo + rows, cols].astype(F32), rim_k, short[1, :, cols])
        v = conv3(v_mr[lo : lo + rows, cols].astype(F32), rim_v, short[2, :, cols])
        u_own[lo : lo + rows, cols] = (k * v).astype(BF)

    def before(stream, lo, cols):
        return stream[lo - 16 : lo, cols].astype(F32)[8:]

    def u_late(i):
        cols = cols_of(i)
        u_rows(H, H, cols, before(k_mr, H, cols), before(v_mr, H, cols))

    loop(chunks, u_late)

    pl.semaphore_wait(barrier, n - 1 + mp - 1)

    nxt = {"ctx": lax.rem(ctx + 1, n)}
    rim_copy = pltpu.make_async_remote_copy(pack, rims, rim_s, rim_r, device_id=nxt, device_id_type=MESH)
    halo_copy = pltpu.make_async_remote_copy(
        u_own.at[pl.ds(H, H)], u_halo, halo_s, halo_r, device_id=nxt, device_id_type=MESH
    )
    nr_copy = pltpu.make_async_remote_copy(
        nbuf.at[pl.ds(T - 16, 16)], nrim, nr_s, nr_r, device_id=nxt, device_id_type=MESH
    )

    @pl.when(not_last)
    def _():
        rim_copy.start()
        halo_copy.start()

    def mr_spec(i):
        cols = cols_of(i)
        store_spectrum(spec1, dot3(f1h[:, 0:H], f1l[:, 0:H], mr_taps[:, cols]), H, cols)

    need(6, 10, 11)
    loop(chunks, mr_spec)

    @pl.when(not_first)
    def _():
        rim_copy.wait_recv()

    def rim_of(s, cols):
        both = rims[:, cols].astype(F32)
        part = both[0:8] if s < 4 else both[8:16]
        by = (6 - 2 * s) % 8
        return pltpu.roll(part, by, 0) if by else part

    def u_early(i):
        cols = cols_of(i)
        u_rows(0, H, cols, rim_of(1, cols), rim_of(2, cols))

    loop(chunks, u_early)

    def mr_half(part):
        acc_ss[...] = jnp.zeros(acc_ss.shape, F32)

        def mr_body(i):
            cols = cols_of(i)
            if part == 1:
                win = u_own[:, cols]
                sq = conv3(q_mr[H:T, cols].astype(F32), before(q_mr, H, cols), short[0, :, cols])
            else:
                win = jnp.concatenate([u_halo[:, cols], u_own[0:H, cols]], axis=0)
                sq = conv3(q_mr[0:H, cols].astype(F32), rim_of(0, cols), short[0, :, cols])
            u = dot(f1h[...], win) + dot(f1l[...], win)
            y = dot3(g1h[...], g1l[...], spectrum_product(u, spec1[:, cols], T // 2))
            m = (sq * y).astype(BF)
            out_mr[part * H : part * H + H, cols] = m
            w = m.astype(F32)
            w = w * w
            acc_ss[...] += w[:, 0:128] + w[:, 128:256]

        loop(chunks, mr_body)
        row = jnp.sum(acc_ss[...].T, axis=0, keepdims=True)
        ss[part, mpi] = jnp.broadcast_to(row, (8, H))

    def ss_copy(part, j, slot):
        return pltpu.make_async_remote_copy(
            ss.at[part, slot], ss.at[part, slot], ss_s.at[part, j], ss_r.at[part, slot],
            device_id={"mp": lax.rem(mpi + j, mp)}, device_id_type=MESH,
        )

    def ss_send(part):
        for j in range(1, mp):
            ss_copy(part, j, mpi).start()

    def norm_half(part):
        for j in range(1, mp):
            ss_copy(part, j, lax.rem(mpi + j, mp)).wait_recv()
        total = ss[part, 0]
        for j in range(1, mp):
            total = total + ss[part, j]
        sc = lax.rsqrt(total / (C * mp) + 1e-06)
        scale[...] = jnp.broadcast_to(sc[0:1], (H, H)).T

        def norm_body(i):
            cols = cols_of(i)
            s = scale[...]
            s = jnp.concatenate([s, s], axis=1)
            m = out_mr[part * H : part * H + H, cols].astype(F32)
            nbuf[part * H : part * H + H, cols] = (m * s * gain[0:1, cols]).astype(BF)

        loop(chunks, norm_body)

    need(12, 13)
    mr_half(1)
    ss_send(1)

    def li_gates(i):
        cols = cols_of(i)
        lkb[:, cols] = conv3(k_li[:, cols].astype(F32), rim_of(4, cols), short[4, :, cols])
        lqb[:, cols] = conv3(q_li[:, cols].astype(F32), rim_of(3, cols), short[3, :, cols])

    loop(chunks, li_gates)

    need(7, 8, 9, 14)
    norm_half(1)

    @pl.when(not_last)
    def _():
        nr_copy.start()

    x = 2.0 * rate[...]
    series = x * (1.0 + x * (-1.0 / 2 + x * (1.0 / 6 + x * (-1.0 / 24 + x * (1.0 / 120 - x * (1.0 / 720))))))
    wgt[...] = res[...] * jnp.sqrt(jnp.where(x < 0.125, series, 1.0 - jnp.exp(-x)))

    sub = lax.broadcasted_iota(jnp.int32, (8, 128), 0).astype(F32)

    def rows_of(ref, cols):
        return [jnp.broadcast_to(ref[m : m + 1, cols], (8, 128)) for m in range(modes)]

    def tree(vals):
        vals = list(vals)
        while len(vals) > 1:
            vals = [a + b for a, b in zip(vals[0::2], vals[1::2])] + ([vals[-1]] if len(vals) % 2 else [])
        return vals[0]

    def h_group(i):
        cols = cols_of(i, 128)
        r = rows_of(rate, cols)
        w = rows_of(wgt, cols)
        d8 = [jnp.exp(-8.0 * a) for a in r]
        g = tuple(b * jnp.exp(-a * sub) for a, b in zip(r, w))

        def step(k, g):
            hbuf[pl.ds(pl.multiple_of(k * 8, 8), 8), cols] = tree(g)
            return tuple(a * b for a, b in zip(g, d8))

        lax.fori_loop(0, H // 8, step, g, unroll=4)

    loop(C // 128, h_group)

    def li_spec(i):
        cols = cols_of(i)
        store_spectrum(spec2, dot3(f1h[:, 0:H], f1l[:, 0:H], hbuf[:, cols]), H, cols)

    loop(chunks, li_spec)

    @pl.when(not_first)
    def _():
        halo_copy.wait_recv()

    mr_half(0)
    ss_send(0)

    E = H + 16

    def li_u_late(i):
        cols = cols_of(i)
        lv = conv3(nbuf[E:T, cols].astype(F32), nbuf[H:E, cols].astype(F32)[8:], short[5, :, cols])
        u32[E:T, cols] = (lkb[E:T, cols] * lv).astype(BF).astype(F32)

    loop(chunks, li_u_late)

    def horner(lo, hi, acc, d8, cols):
        def step(k, acc):
            u = u32[pl.ds(pl.multiple_of(k * 8, 8), 8), cols]
            return tuple(a * d + u for a, d in zip(acc, d8))

        return lax.fori_loop(lo // 8, hi // 8, step, acc, unroll=2)

    def zeros8():
        return tuple(jnp.zeros((8, 128), F32) for _ in range(modes))

    def ends_late(i):
        cols = cols_of(i, 128)
        d8 = [jnp.exp(-8.0 * a) for a in rows_of(rate, cols)]
        acc = horner(E, T, zeros8(), d8, cols)
        for m in range(modes):
            late[8 * m : 8 * m + 8, cols] = acc[m]

    loop(C // 128, ends_late)
    norm_half(0)

    @pl.when(not_first)
    def _():
        nr_copy.wait_recv()

    def li_u(i):
        cols = cols_of(i)
        lv = conv3(nbuf[0:E, cols].astype(F32), nrim[:, cols].astype(F32)[8:], short[5, :, cols])
        u32[0:E, cols] = (lkb[0:E, cols] * lv).astype(BF).astype(F32)

    loop(chunks, li_u)

    def ends_group(i):
        cols = cols_of(i, 128)
        r = rows_of(rate, cols)
        d8 = [jnp.exp(-8.0 * a) for a in r]
        place = [jnp.exp(-a * (7.0 - sub)) for a in r]
        acc = horner(0, H, zeros8(), d8, cols)
        for m in range(modes):
            emid[m : m + 1, cols] = jnp.sum(acc[m] * place[m], axis=0, keepdims=True)
        acc = horner(H, E, acc, d8, cols)
        for m in range(modes):
            whole = acc[m] * jnp.exp(-float(T - E) * r[m]) + late[8 * m : 8 * m + 8, cols]
            ebuf[m : m + 1, cols] = jnp.sum(whole * place[m], axis=0, keepdims=True)

    loop(C // 128, ends_group)
    st[ctx] = ebuf[...].astype(BF)

    def st_copy(dst, slot):
        return pltpu.make_async_remote_copy(
            st.at[slot], st.at[slot], st_s.at[dst], st_r.at[slot], device_id={"ctx": dst}, device_id_type=MESH
        )

    def st_start(j, c):
        st_copy(j, ctx).start()
        return c

    lax.fori_loop(ctx + 1, n, st_start, 0)

    def li_local(i):
        cols = cols_of(i)
        win = jnp.concatenate([u32[0:H, cols], u32[H:T, cols]], axis=1).astype(BF)
        u = dot(fcat[...], jnp.concatenate([win, win], axis=0))
        spec = spec2[:, cols]
        p = spectrum_product(u, jnp.concatenate([spec, spec], axis=1), H)
        y = dot3(g1h[...], g1l[...], p)
        ylong[0:H, cols] = y[:, :CW]
        ylong[H:T, cols] = y[:, CW:]

    loop(chunks, li_local)

    carry[...] = jnp.zeros(carry.shape, F32)

    def st_take(j, c):
        st_copy(lax.rem(ctx + 1, n), j).wait_recv()
        carry[...] = carry[...] * jnp.exp(-float(T) * rate[...]) + st[j].astype(F32)
        return c

    lax.fori_loop(0, ctx, st_take, 0)

    def out_group(i):
        cols = cols_of(i, 128)
        r = rows_of(rate, cols)
        w = rows_of(wgt, cols)
        s = rows_of(carry, cols)
        d8 = [jnp.exp(-8.0 * a) for a in r]
        start = [b * jnp.exp(-a * (sub + 1.0)) for a, b in zip(r, w)]

        def step(k, g):
            rows = pl.ds(pl.multiple_of(k * 16, 16), 16)
            y0 = tree(g)
            g = tuple(a * b for a, b in zip(g, d8))
            y1 = tree(g)
            g = tuple(a * b for a, b in zip(g, d8))
            y = ylong[rows, cols] + jnp.concatenate([y0, y1], axis=0)
            out_li[rows, cols] = (lqb[rows, cols] * y.astype(BF).astype(F32)).astype(BF)
            return g

        lax.fori_loop(0, H // 16, step, tuple(a * b for a, b in zip(start, s)), unroll=2)
        mid = rows_of(emid, cols)
        s = [a * jnp.exp(-float(H) * b) + c for a, b, c in zip(s, r, mid)]
        lax.fori_loop(H // 16, T // 16, step, tuple(a * b for a, b in zip(start, s)), unroll=2)

    loop(C // 128, out_group)

    @pl.when(not_last)
    def _():
        rim_copy.wait_send()
        halo_copy.wait_send()
        nr_copy.wait_send()

    for part in range(2):
        for j in range(1, mp):
            ss_copy(part, j, mpi).wait_send()

    def st_end(j, c):
        st_copy(j, ctx).wait_send()
        return c

    lax.fori_loop(ctx + 1, n, st_end, 0)


def shards(n, mp, q_mr, k_mr, v_mr, q_li, k_li, short_taps, mr_taps, norm_gain, decay_rate, residue):
    T, C = q_mr.shape
    modes = decay_rate.shape[0]
    (f1h, f1l), (g1h, g1l) = dft_tables(T, T // 2, T)
    fcat = np.concatenate([f1h[:, T // 2 :], f1l[:, T // 2 :]], axis=1)
    args = [q_mr, k_mr, v_mr, q_li, k_li, short_taps, mr_taps, norm_gain[None], decay_rate, residue]
    args += [jnp.asarray(a) for a in (f1h, f1l, g1h, g1l, fcat)]
    vm = pl.BlockSpec(memory_space=pltpu.VMEM)
    DMA = pltpu.SemaphoreType.DMA
    H = T // 2
    return pl.pallas_call(
        functools.partial(kernel, n, mp),
        out_shape=(jax.ShapeDtypeStruct((T, C), BF), jax.ShapeDtypeStruct((T, C), BF)),
        in_specs=[pl.BlockSpec(memory_space=pltpu.HBM)] * IN,
        out_specs=(vm, vm),
        scratch_shapes=[pltpu.VMEM(a.shape, a.dtype) for a in args]
        + [
            DMA((IN,)),
            pltpu.VMEM((T, C), BF),
            pltpu.VMEM((H, C), BF),
            pltpu.VMEM((16, C), BF),
            pltpu.VMEM((16, C), BF),
            pltpu.VMEM((T + 8, C), F32),
            pltpu.VMEM((T + 8, C), F32),
            pltpu.VMEM((H, C), F32),
            pltpu.VMEM((T, C), F32),
            pltpu.VMEM((T, C), F32),
            pltpu.VMEM((T, C), BF),
            pltpu.VMEM((16, C), BF),
            pltpu.VMEM((T, C), F32),
            pltpu.VMEM((T, C), F32),
            pltpu.VMEM((modes, C), F32),
            pltpu.VMEM((modes, C), F32),
            pltpu.VMEM((modes, C), F32),
            pltpu.VMEM((8 * modes, C), F32),
            pltpu.VMEM((modes, C), F32),
            pltpu.VMEM((n, modes, C), BF),
            pltpu.VMEM((2, mp, 8, H), F32),
            pltpu.VMEM((H, H), F32),
            pltpu.VMEM((H, 128), F32),
            DMA, DMA, DMA, DMA, DMA, DMA,
            DMA((2, mp)), DMA((2, mp)), DMA((n,)), DMA((n,)),
        ],
        compiler_params=pltpu.CompilerParams(
            collective_id=0, has_side_effects=True, vmem_limit_bytes=56 * 1024 * 1024
        ),
    )(*args)


def solution(mesh):
    n, mp = mesh.shape["ctx"], mesh.shape["mp"]
    tok = P("ctx", "mp")
    in_specs = (tok,) * 5 + (P(None, None, "mp"), P(None, "mp"), P("mp"), P(None, "mp"), P(None, "mp"))
    return jax.shard_map(
        functools.partial(shards, n, mp), mesh=mesh, in_specs=in_specs, out_specs=(tok, tok), check_vma=False
    )
```
